512 devices in a mesh: dp: 32 (over y_hi, z), tensor: 16 (over x, y_lo, core).
Axes of the slice: x: 4, y: 4 (y_hi: 2, y_lo: 2; y = y_hi * 2 + y_lo), z: 16, core: 2. Of those that a mesh axis runs over, the one named last changes fastest.
Arguments:
- cotangent: bfloat16 [4096, 4096], P('dp', 'tensor'), may hold values from -6 to 6
- gate_pre: bfloat16 [4096, 14336], P('dp', 'tensor'), may hold values from -6 to 6
- up_pre: bfloat16 [4096, 14336], P('dp', 'tensor'), may hold values from -6 to 6
- down_weight: bfloat16 [14336, 4096], P('tensor', 'dp'), may hold values from -0.046875 to 0.046875
Outputs:
- grad_gate: bfloat16 [4096, 14336], P('dp', 'tensor')
- grad_up: bfloat16 [4096, 14336], P('dp', 'tensor')
- grad_down: float32 [14336, 4096], P('tensor', 'dp')
The draws below stay inside these ranges and needn't reach their ends.
All inputs are finite; a program needn't handle non-finite values.
Results may differ from the reference program's by a relative error of at most 0.003.
Values may be sent and summed in bfloat16 or wider, within the bound.
A program may use at most 64 MiB of HBM per device.

```python
import jax
import jax.numpy as jnp

D = 4096
FF = 14336
TOKENS = 4096


def with_spikes(drawn, key, source, target, shards_of, factor):
    owner, partner = [(jnp.arange(drawn.shape[axis_at]) // (drawn.shape[axis_at] // shards_of)).reshape([-1 if axis == axis_at else 1 for axis in range(drawn.ndim)]) for axis_at in (source, target)]
    chosen = jax.random.permutation(key, shards_of)[partner]
    strong = (owner == chosen) | (owner == (partner + shards_of // 2) % shards_of)
    return jnp.where(strong, factor * drawn, drawn)


def steps_of(own_key, extent, shards, least, top_value):
    def one(position, parts):
        steps = jax.random.uniform(jax.random.fold_in(jax.random.fold_in(own_key, 6), position), (parts,), jnp.float32, least / len(shards), top_value / len(shards))
        return jnp.repeat(jnp.exp(steps), extent[position] // parts).reshape((-1,) + (1,) * (len(extent) - position - 1))

    gain = one(*shards[0])
    for cut in shards[1:]:
        gain = gain * one(*cut)
    return gain


def noise(own_key, extent, spread, reach, pieces=(), held_as=jnp.bfloat16):
    result = spread * jax.random.normal(own_key, extent, jnp.float32)
    if pieces:
        result = result * steps_of(own_key, extent, pieces, -0.22, 0.18)
    return jnp.clip(result, -reach, reach).astype(held_as)


def bell_draw_with(key, shape, scale, reach, split, heavy, held_as=jnp.bfloat16):
    drawn = scale * jax.random.normal(key, shape, jnp.float32)
    if split:
        drawn = drawn * steps_of(key, shape, split, -0.22, 0.18)
    return jnp.clip(with_spikes(drawn, jax.random.fold_in(key, 3), *heavy), -reach, reach).astype(held_as)


def setup_inputs(seed: int = 0) -> dict:
    key_of = jax.random.split(jax.random.key(seed), 5)
    cotangent = bell_draw_with(key_of[0], (TOKENS, D), 1.0, 6.0, ((0, 32), (1, 16)), (0, 1, 32, 2.75))
    gate_pre = noise(key_of[1], (TOKENS, FF), 1.0, 6.0, ((0, 32), (1, 16)))
    up_pre = noise(key_of[2], (TOKENS, FF), 1.0, 6.0, ((0, 32), (1, 16)))
    down_weight = noise(key_of[3], (FF, D), FF ** -0.5, 0.046875, ((0, 16), (1, 32)))
    return dict(cotangent=cotangent, gate_pre=gate_pre, up_pre=up_pre, down_weight=down_weight)


def reference(cotangent, gate_pre, up_pre, down_weight):
    gate_vals = gate_pre.astype(jnp.float32)
    up_vals = up_pre.astype(jnp.float32)
    sigma = jax.nn.sigmoid(gate_vals)
    act_vals = gate_vals * sigma
    hidden = (act_vals * up_vals).astype(jnp.bfloat16)
    dhid = jnp.dot(cotangent, down_weight.T, preferred_element_type=jnp.float32)
    grad_up = (dhid * act_vals).astype(jnp.bfloat16)
    grad_gate = (dhid * up_vals * sigma * (1.0 + gate_vals * (1.0 - sigma))).astype(jnp.bfloat16)
    grad_down = jnp.dot(hidden.T, cotangent, preferred_element_type=jnp.float32) * (TOKENS ** -0.5)
    return grad_gate, grad_up, grad_down
```

```python
import jax
import jax.numpy as jnp
from jax import lax
from jax.experimental import pallas as pl
from jax.experimental.pallas import tpu as pltpu
from jax.sharding import PartitionSpec as P

MESH = pl.DeviceIdType.MESH
F32, BF16 = jnp.float32, jnp.bfloat16
NX, NZ = 4, 16
NK = NZ // 2
B = 128
FD = 896
R = FD // NK
RS = NX * R
NC, CH = 4, 256

GRAD_SUM = BF16
GRAD_BACK = F32
DOWN_SUM = BF16
DOWN_BACK = BF16


def kernel(cot, gate, up, weight, o_gate, o_up, o_down,
           hid_t, f_up, f_gate, cot_b, w_g, h_g,
           d_f, d_p, d_r, d_s, d_own,
           g_f, g_p, g_r, g_s, g_own,
           sem_ring_r, sem_ring_l, sem_d, sem_g, sem):
    i, j = lax.axis_index("dp"), lax.axis_index("tensor")
    yh, z = i // NZ, i % NZ
    x, yl, c = j // 4, (j // 2) % 2, j % 2
    y = yh * 2 + yl
    par = (z + yl) % 2
    me = i * 16 + j

    def dev(x, yh, yl, z, c):
        return yh * NZ + z, x * 4 + yl * 2 + c

    def is_me(d):
        return d[0] * 16 + d[1] == me

    names = ["cot_send", "cot_recv", "w_send", "w_recv", "h_send", "h_recv", "ring_send_r", "ring_send_l",
             "sib_send", "sib_recv", "wg_send", "wg_recv", "hg_send", "hg_recv", "ds_send", "gs_send",
             "db_send", "db_recv", "gb_send", "gb_recv"]
    sems = {n: sem.at[k] for k, n in enumerate(names)}

    def remote(src, dst, send, recv, d):
        return pltpu.make_async_remote_copy(
            src_ref=src, dst_ref=dst, send_sem=send, recv_sem=recv, device_id=d, device_id_type=MESH)

    def send_any(src, dst, send, recv, d):
        @pl.when(is_me(d))
        def _():
            pltpu.make_async_copy(src, dst, recv).start()

        @pl.when(jnp.logical_not(is_me(d)))
        def _():
            remote(src, dst, send, recv, d).start()

    def wait(ref, s):
        pltpu.make_async_copy(ref, ref, s).wait()

    h_dst = [dev(x, yh, z % 2, 2 * s + c, yl) for s in range(NK)]
    w_dst = [dev(2 * yh + z % 2, x // 2, x % 2, 2 * s + c, yl) for s in range(NK)]
    c_dst = [dev(2 * (x // 2) + e, yh, z % 2, z, c) for e in range(2)]
    h_src = [dev(x, yh, c, 2 * k + yl, z % 2) for k in range(NK)]
    w_src = [dev(y, x // 2, c, 2 * k + x % 2, z % 2) for k in range(NK)]
    c_src = [dev(2 * (x // 2) + a, yh, b, z, c) for a in range(2) for b in range(2)]
    right, left = dev(x, yh, yl, (z + 1) % NZ, c), dev(x, yh, yl, (z + NZ - 1) % NZ, c)
    sibling = dev(x, yh, yl, z, 1 - c)
    x_dst = [dev((x + o) % 4, yh, yl, z, c) for o in range(1, 4)]
    y_idx = [(y + o) % 4 for o in range(1, 4)]
    y_dst = [dev(x, v // 2, v % 2, z, c) for v in y_idx]

    barrier = pltpu.get_barrier_semaphore()

    def greet(d):
        pl.semaphore_signal(barrier, inc=1, device_id=d, device_id_type=MESH)

    for d in h_src + w_src:
        @pl.when(jnp.logical_not(is_me(d)))
        def _():
            greet(d)
    for d in c_src:
        @pl.when(jnp.logical_and(par == 0, jnp.logical_not(is_me(d))))
        def _():
            greet(d)
    for d in [right, left, sibling] + x_dst + y_dst:
        greet(d)

    for b in range(FD // 128):
        cols = slice(b * 128, (b + 1) * 128)
        g, u = gate[:, cols].astype(F32), up[:, cols].astype(F32)
        sig = jax.nn.sigmoid(g)
        act = g * sig
        f_up[:, cols] = act
        f_gate[:, cols] = u * sig * (1.0 + g * (1.0 - sig))
        hid_t[cols, :] = (act * u).T.astype(BF16)

    def others(dsts):
        n = jnp.int32(0)
        for d in dsts:
            n = n + jnp.where(is_me(d), 0, 1)
        return n

    n_h, n_w, n_c = others(h_dst), others(w_dst), others(c_dst)
    pl.semaphore_wait(barrier, n_h + n_w + n_c + 9)

    for e in range(2):
        send_any(cot.at[:, pl.ds(e * B, B)],
                 cot_b.at[c * 2 + x % 2, pl.ds((z // 2) * B, B), pl.ds(yl * B, B)],
                 sems["cot_send"], sems["cot_recv"], c_dst[e])
    kz = z // 2
    for s in range(NK):
        send_any(weight.at[pl.ds(s * R, R)],
                 w_g.at[(kz % 2) * 2 + kz // 4, pl.ds(x * R, R), pl.ds(((kz // 2) % 2) * B, B)],
                 sems["w_send"], sems["w_recv"], w_dst[s])

    def send_hidden():
        for s in range(NK):
            send_any(hid_t.at[pl.ds(s * R, R)],
                     h_g.at[kz // 2, pl.ds(x * R, R), pl.ds((kz % 2) * B, B)],
                     sems["h_send"], sems["h_recv"], h_dst[s])

    def panel(zt):
        return cot_b.at[pl.ds(2 * c, 2), pl.ds(((zt + 2 * NZ) % NZ) // 2 * B, B)]

    def forward(ref, d, send, recv):
        remote(ref, ref, send, recv, d).start()

    for t in range(4):
        dist = 2 * t + par
        if t == 0:
            @pl.when(par == 0)
            def _():
                wait(panel(z), sems["cot_recv"])

            @pl.when(par == 1)
            def _():
                wait(panel(z - dist), sem_ring_r.at[0])
                wait(panel(z + dist), sem_ring_l.at[0])
        else:
            wait(panel(z - dist), sem_ring_r.at[t])
            wait(panel(z + dist), sem_ring_l.at[t])
        forward(panel(z - dist), right, sems["ring_send_r"], sem_ring_r.at[t + par])
        if t < 3:
            forward(panel(z + dist), left, sems["ring_send_l"], sem_ring_l.at[t + par])
        else:
            @pl.when(par == 0)
            def _():
                forward(panel(z + dist), left, sems["ring_send_l"], sem_ring_l.at[t])
        forward(panel(z - dist), sibling, sems["sib_send"], sems["sib_recv"])
        if t > 0:
            forward(panel(z + dist), sibling, sems["sib_send"], sems["sib_recv"])
        else:
            @pl.when(par == 1)
            def _():
                forward(panel(z + dist), sibling, sems["sib_send"], sems["sib_recv"])
        if t == 0:
            send_hidden()

    @pl.when(par == 0)
    def _():
        wait(panel(z - 8), sem_ring_r.at[4])
        forward(panel(z - 8), sibling, sems["sib_send"], sems["sib_recv"])

    mine_w = w_g.at[:, pl.ds(y * R, R)]
    mine_h = h_g.at[:, pl.ds(x * R, R)]
    three = h_g.at[:, pl.ds(0, 3 * R)]
    wait(mine_w, sems["w_recv"])
    for d in y_dst:
        forward(mine_w, d, sems["wg_send"], sems["wg_recv"])
    wait(mine_h, sems["h_recv"])
    for d in x_dst:
        forward(mine_h, d, sems["hg_send"], sems["hg_recv"])

    wait(cot_b.at[pl.ds(2 * (1 - c), 2)], sems["sib_recv"])
    wait(three, sems["wg_recv"])

    @pl.loop(0, NC)
    def _(n):
        rows = pl.ds(pl.multiple_of(n * CH, CH), CH)
        total = jnp.zeros((RS, CH), F32)
        for q in range(NC):
            total += lax.dot_general(w_g[q], cot_b[q, rows, :], (((1,), (1,)), ((), ())),
                                     preferred_element_type=F32)
        d_f[n] = total
        for v in range(NX):
            d_p[v, n] = total[v * R:(v + 1) * R].astype(GRAD_SUM)
        for o in range(1, 4):
            remote(d_p.at[(x + o) % 4, n], d_r.at[o - 1, n], sems["ds_send"], sem_d.at[n], x_dst[o - 1]).start()

    wait(three, sems["hg_recv"])

    @pl.loop(0, NC)
    def _(n):
        total = jnp.zeros((RS, CH), F32)
        for q in range(NC):
            total += jnp.dot(h_g[q], cot_b[n, q * CH:(q + 1) * CH, :], preferred_element_type=F32)
        g_f[n] = total
        for v in range(NX):
            g_p[v, n] = total[v * R:(v + 1) * R].astype(DOWN_SUM)
        for o in range(1, 4):
            remote(g_p.at[y_idx[o - 1], n], g_r.at[o - 1, n], sems["gs_send"], sem_g.at[n], y_dst[o - 1]).start()

    back = pl.ds(pl.multiple_of((z // 2) * R, R), R)
    for n in range(NC):
        wait(d_r.at[:, n], sem_d.at[n])
        total = d_f[n, pl.ds(pl.multiple_of(x * R, R), R), :]
        for o in range(3):
            total += d_r[o, n].astype(F32)
        for a in range(2):
            k = 2 * n + a
            d_s[k] = total[:, a * B:(a + 1) * B].astype(GRAD_BACK)
            send_any(d_s.at[k], d_own.at[back], sems["db_send"], sems["db_recv"], h_src[k])
    for n in range(NC):
        wait(g_r.at[:, n], sem_g.at[n])
        total = g_f[n, pl.ds(pl.multiple_of(y * R, R), R), :]
        for o in range(3):
            total += g_r[o, n].astype(F32)
        for a in range(2):
            k = 4 * (n % 2) + 2 * a + n // 2
            g_s[k] = total[:, a * B:(a + 1) * B].astype(DOWN_BACK)
            send_any(g_s.at[k], g_own.at[back], sems["gb_send"], sems["gb_recv"], w_src[k])

    wait(d_own, sems["db_recv"])
    for b in range(FD // 128):
        cols = slice(b * 128, (b + 1) * 128)
        dhid = d_own[cols, :].astype(F32).T
        o_up[:, cols] = (dhid * f_up[:, cols]).astype(BF16)
        o_gate[:, cols] = (dhid * f_gate[:, cols]).astype(BF16)
    wait(g_own, sems["gb_recv"])
    scale = 1.0 / 64.0
    o_down[...] = g_own[...].astype(F32) * scale

    def wait_all(ref, s, count, most):
        for k in (most - 1, most):
            @pl.when(count == k)
            def _():
                wait(ref.at[pl.ds(0, k)], s)

    def wait_rows(ref, s, count):
        for k in (NK - 1, NK):
            @pl.when(count == k)
            def _():
                wait(ref.at[pl.ds(0, k * R)], s)

    for k in (1, 2):
        @pl.when(n_c == k)
        def _():
            wait(cot.at[:, pl.ds(0, k * B)], sems["cot_send"])
    wait_rows(weight, sems["w_send"], n_w)
    wait_rows(hid_t, sems["h_send"], n_h)
    wait(cot_b.at[pl.ds(0, 2), pl.ds(0, 4 * B)], sems["ring_send_r"])

    @pl.when(par == 0)
    def _():
        wait(cot_b.at[pl.ds(0, 2), pl.ds(0, 4 * B)], sems["ring_send_l"])

    @pl.when(par == 1)
    def _():
        wait(cot_b.at[pl.ds(0, 2), pl.ds(0, 3 * B)], sems["ring_send_l"])

    wait(cot_b.at[pl.ds(0, 2)], sems["sib_send"])
    wait(three, sems["wg_send"])
    wait(three, sems["hg_send"])
    wait(d_r, sems["ds_send"])
    wait(g_r, sems["gs_send"])
    wait_all(d_s, sems["db_send"], n_h, NK)
    wait_all(g_s, sems["gb_send"], n_w, NK)


def shards(cotangent, gate_pre, up_pre, down_weight):
    vmem = pl.BlockSpec(memory_space=pltpu.VMEM)
    dma = pltpu.SemaphoreType.DMA
    return pl.pallas_call(
        kernel,
        name="swiglu_down_backward",
        out_shape=(
            jax.ShapeDtypeStruct((B, FD), BF16),
            jax.ShapeDtypeStruct((B, FD), BF16),
            jax.ShapeDtypeStruct((FD, B), F32),
        ),
        in_specs=[vmem] * 4,
        out_specs=(vmem,) * 3,
        scratch_shapes=[
            pltpu.VMEM((FD, B), BF16),
            pltpu.VMEM((B, FD), F32),
            pltpu.VMEM((B, FD), F32),
            pltpu.VMEM((NC, NK * B, CH), BF16),
            pltpu.VMEM((NC, RS, CH), BF16),
            pltpu.VMEM((NC, RS, CH), BF16),
            pltpu.VMEM((NC, RS, CH), F32),
            pltpu.VMEM((NX, NC, R, CH), GRAD_SUM),
            pltpu.VMEM((3, NC, R, CH), GRAD_SUM),
            pltpu.VMEM((NK, R, B), GRAD_BACK),
            pltpu.VMEM((FD, B), GRAD_BACK),
            pltpu.VMEM((NC, RS, CH), F32),
            pltpu.VMEM((NX, NC, R, CH), DOWN_SUM),
            pltpu.VMEM((3, NC, R, CH), DOWN_SUM),
            pltpu.VMEM((NK, R, B), DOWN_BACK),
            pltpu.VMEM((FD, B), DOWN_BACK),
            dma((5,)), dma((4,)), dma((NC,)), dma((NC,)), dma((20,)),
        ],
        compiler_params=pltpu.CompilerParams(
            collective_id=0, has_side_effects=True, vmem_limit_bytes=48 * 2**20),
        cost_estimate=pl.CostEstimate(flops=4 * RS * 1024 * 1024, bytes_accessed=2 * 2**20, transcendentals=B * FD),
    )(cotangent, gate_pre, up_pre, down_weight)


def solution(mesh):
    in_specs = (P("dp", "tensor"), P("dp", "tensor"), P("dp", "tensor"), P("tensor", "dp"))
    out_specs = (P("dp", "tensor"), P("dp", "tensor"), P("tensor", "dp"))
    return jax.shard_map(shards, mesh=mesh, in_specs=in_specs, out_specs=out_specs, check_vma=False)
```

```python
import jax
import jax.numpy as jnp
from jax import lax
from jax.experimental import pallas as pl
from jax.experimental.pallas import tpu as pltpu
from jax.sharding import PartitionSpec as P

MESH = pl.DeviceIdType.MESH
F32, BF16 = jnp.float32, jnp.bfloat16
NX, NZ = 4, 16
NK = NZ // 2
B = 128
FD = 896
R = FD // NK
RS = NX * R
NC, CH = 4, 256

NP, PR = 2, B // 2
W_AT, H_AT = 1, 2

AHEAD = 2
W_FIRST = False
PASS_AT = 3

GRAD_SUM = BF16
GRAD_BACK = F32
DOWN_SUM = BF16
DOWN_BACK = BF16


def kernel(cot_in, gate_in, up_in, weight_in, o_gate, o_up, o_down,
           cot, gate, up, weight, hid_t, f_up, f_gate, cot_b, w_g, h_g,
           d_f, d_p, d_r, d_s, d_own,
           g_f, g_p, g_r, g_s, g_own,
           sem_near, sem_ring_r, sem_ring_l, sem_w, sem_h, sem_d, sem_g, sem_in, sem):
    i, j = lax.axis_index("dp"), lax.axis_index("tensor")
    yh, z = i // NZ, i % NZ
    x, yl, c = j // 4, (j // 2) % 2, j % 2
    y = yh * 2 + yl
    par = (z + yl) % 2
    me = i * 16 + j

    def dev(x, yh, yl, z, c):
        return yh * NZ + z, x * 4 + yl * 2 + c

    def is_me(d):
        return d[0] * 16 + d[1] == me

    names = ["cot_send", "w_send", "h_send", "ring_send_r", "ring_send_l",
             "sib_send", "sib_recv", "wg_send", "wg_recv", "hg_send", "hg_recv", "ds_send", "gs_send",
             "db_send", "db_recv", "gb_send", "gb_recv"]
    sems = {n: sem.at[k] for k, n in enumerate(names)}

    def remote(src, dst, send, recv, d):
        return pltpu.make_async_remote_copy(
            src_ref=src, dst_ref=dst, send_sem=send, recv_sem=recv, device_id=d, device_id_type=MESH)

    def send_any(src, dst, send, recv, d):
        @pl.when(is_me(d))
        def _():
            pltpu.make_async_copy(src, dst, recv).start()

        @pl.when(jnp.logical_not(is_me(d)))
        def _():
            remote(src, dst, send, recv, d).start()

    def wait(ref, s):
        pltpu.make_async_copy(ref, ref, s).wait()

    h_dst = [dev(x, yh, z % 2, 2 * s + c, yl) for s in range(NK)]
    w_dst = [dev(2 * yh + z % 2, x // 2, x % 2, 2 * s + c, yl) for s in range(NK)]
    near = (0, 1, -1, 2, -2)
    c_dst = [(o, e, dev(2 * (x // 2) + e, yh, z % 2, (z + o + NZ) % NZ, c)) for o in near for e in range(2)]
    h_src = [dev(x, yh, c, 2 * k + yl, z % 2) for k in range(NK)]
    w_src = [dev(y, x // 2, c, 2 * k + x % 2, z % 2) for k in range(NK)]
    c_src = [(abs(o) % 2, dev(2 * (x // 2) + a, yh, b, (z + o + NZ) % NZ, c))
             for o in near for a in range(2) for b in range(2)]
    right, left = dev(x, yh, yl, (z + 1) % NZ, c), dev(x, yh, yl, (z + NZ - 1) % NZ, c)
    right2, left2 = dev(x, yh, yl, (z + 2) % NZ, c), dev(x, yh, yl, (z + NZ - 2) % NZ, c)
    sibling = dev(x, yh, yl, z, 1 - c)
    x_dst = [dev((x + o) % 4, yh, yl, z, c) for o in range(1, 4)]
    y_idx = [(y + o) % 4 for o in range(1, 4)]
    y_dst = [dev(x, v // 2, v % 2, z, c) for v in y_idx]

    loads = [pltpu.make_async_copy(a, b, sem_in.at[k])
             for k, (a, b) in enumerate([(gate_in, gate), (up_in, up), (cot_in, cot), (weight_in, weight)])]
    for load in loads:
        load.start()

    barrier = pltpu.get_barrier_semaphore()

    def greet(d):
        pl.semaphore_signal(barrier, inc=1, device_id=d, device_id_type=MESH)

    for d in h_src + w_src:
        @pl.when(jnp.logical_not(is_me(d)))
        def _():
            greet(d)
    for odd, d in c_src:
        @pl.when(jnp.logical_and(par == odd, jnp.logical_not(is_me(d))))
        def _():
            greet(d)
    for d in [right, left, right2, left2, sibling] + x_dst + y_dst:
        greet(d)

    loads[0].wait()
    loads[1].wait()
    for b in range(FD // 128):
        cols = slice(b * 128, (b + 1) * 128)
        g, u = gate[:, cols].astype(F32), up[:, cols].astype(F32)
        sig = jax.nn.sigmoid(g)
        act = g * sig
        hid_t[cols, :] = (act * u).T.astype(BF16)

    def others(dsts):
        n = jnp.int32(0)
        for d in dsts:
            n = n + jnp.where(is_me(d), 0, 1)
        return n

    loads[2].wait()
    loads[3].wait()
    n_h, n_w, n_c = others(h_dst), others(w_dst), others([d for _, _, d in c_dst])
    pl.semaphore_wait(barrier, n_h + n_w + n_c + 11)

    kz = z // 2

    def send_cot():
        for o, e, d in c_dst:
            send_any(cot.at[:, pl.ds(e * B, B)],
                     cot_b.at[c * 2 + x % 2, pl.ds((z // 2) * B, B), pl.ds(yl * B, B)],
                     sems["cot_send"], sem_near.at[o + 2], d)

    def send_weights():
        for s in range(NK):
            send_any(weight.at[pl.ds(s * R, R)],
                     w_g.at[(kz % 2) * 2 + kz // 4, pl.ds(x * R, R), pl.ds(((kz // 2) % 2) * B, B)],
                     sems["w_send"], sem_w.at[kz], w_dst[s])

    if W_FIRST:
        send_weights()
        send_cot()
    else:
        send_cot()
        send_weights()

    def send_hidden():
        for s in range(NK):
            send_any(hid_t.at[pl.ds(s * R, R)],
                     h_g.at[kz // 2, pl.ds(x * R, R), pl.ds((kz % 2) * B, B)],
                     sems["h_send"], sem_h.at[kz], h_dst[s])

    for b in range(FD // 128):
        cols = slice(b * 128, (b + 1) * 128)
        g, u = gate[:, cols].astype(F32), up[:, cols].astype(F32)
        sig = jax.nn.sigmoid(g)
        f_up[:, cols] = g * sig
        f_gate[:, cols] = u * sig * (1.0 + g * (1.0 - sig))

    def panel(zt):
        return cot_b.at[pl.ds(2 * c, 2), pl.ds(((zt + 2 * NZ) % NZ) // 2 * B, B)]

    def forward(ref, d, send, recv):
        remote(ref, ref, send, recv, d).start()

    def piece(zt, q):
        return cot_b.at[pl.ds(2 * c, 2), pl.ds(((zt + 2 * NZ) % NZ) // 2 * B + q * PR, PR)]

    three = h_g.at[:, pl.ds(0, 3 * R)]

    def pass_weights():
        for q in range(NC):
            mine = w_g.at[q, pl.ds(y * R, R)]
            for a in range(2):
                wait(mine.at[:, pl.ds(a * B, B)], sem_w.at[(q % 2) * 4 + 2 * a + q // 2])
            for d in y_dst:
                forward(mine, d, sems["wg_send"], sems["wg_recv"])

    def pass_hidden():
        for q in range(NC):
            mine = h_g.at[q, pl.ds(x * R, R)]
            for a in range(2):
                wait(mine.at[:, pl.ds(a * B, B)], sem_h.at[2 * q + a])
            for d in x_dst:
                forward(mine, d, sems["hg_send"], sems["hg_recv"])

    def to_sibling(zt):
        forward(panel(zt), sibling, sems["sib_send"], sems["sib_recv"])

    def hand_on(zt, d, q, one, two, send, recv):
        forward(piece(zt, q), two, send, recv.at[(d + 2) * NP + q]) if two is not None else None
        forward(piece(zt, q), one, send, recv.at[(d + 1) * NP + q])

    for t in range(4):
        @pl.when(par == 0)
        def _():
            d = 2 * t + 2
            if t == 0:
                wait(panel(z - 2), sem_near.at[4])
                wait(panel(z + 2), sem_near.at[0])
            for q in range(NP):
                if t > 0:
                    wait(piece(z - d, q), sem_ring_r.at[d * NP + q])
                if t < 3:
                    hand_on(z - d, d, q, right, right2, sems["ring_send_r"], sem_ring_r)
                    if t > 0:
                        wait(piece(z + d, q), sem_ring_l.at[d * NP + q])
                    hand_on(z + d, d, q, left, left2 if t < 2 else None, sems["ring_send_l"], sem_ring_l)
            to_sibling(z - d)
            if t < 3:
                to_sibling(z + d)
            if t == 0:
                wait(panel(z), sem_near.at[2])
                to_sibling(z)

        @pl.when(par == 1)
        def _():
            d = 2 * t + 1
            if t == 0:
                wait(panel(z - 1), sem_near.at[3])
                wait(panel(z + 1), sem_near.at[1])
            else:
                for q in range(NP):
                    wait(piece(z - d, q), sem_ring_r.at[d * NP + q])
                    wait(piece(z + d, q), sem_ring_l.at[d * NP + q])
            to_sibling(z - d)
            to_sibling(z + d)

        if t == H_AT:
            send_hidden()
        if t == W_AT:
            pass_weights()

    wait(cot_b.at[pl.ds(2 * (1 - c), 2)], sems["sib_recv"])
    wait(three, sems["wg_recv"])

    def multiply_dhid(n):
        total = jnp.zeros((RS, CH), F32)
        for q in range(NC):
            total += lax.dot_general(w_g[q], cot_b[q, n * CH:(n + 1) * CH, :], (((1,), (1,)), ((), ())),
                                     preferred_element_type=F32)
        d_f[n] = total
        for v in range(NX):
            d_p[v, n] = total[v * R:(v + 1) * R].astype(GRAD_SUM)
        for o in range(1, 4):
            remote(d_p.at[(x + o) % 4, n], d_r.at[o - 1, n], sems["ds_send"], sem_d.at[n], x_dst[o - 1]).start()

    def multiply_down(n):
        total = jnp.zeros((RS, CH), F32)
        for q in range(NC):
            total += jnp.dot(h_g[q], cot_b[n, q * CH:(q + 1) * CH, :], preferred_element_type=F32)
        g_f[n] = total
        for v in range(NX):
            g_p[v, n] = total[v * R:(v + 1) * R].astype(DOWN_SUM)
        for o in range(1, 4):
            remote(g_p.at[y_idx[o - 1], n], g_r.at[o - 1, n], sems["gs_send"], sem_g.at[n], y_dst[o - 1]).start()

    back = pl.ds(pl.multiple_of((z // 2) * R, R), R)

    def reduce_dhid(n):
        wait(d_r.at[:, n], sem_d.at[n])
        total = d_f[n, pl.ds(pl.multiple_of(x * R, R), R), :]
        for o in range(3):
            total += d_r[o, n].astype(F32)
        for a in range(2):
            k = 2 * n + a
            d_s[k] = total[:, a * B:(a + 1) * B].astype(GRAD_BACK)
            send_any(d_s.at[k], d_own.at[back], sems["db_send"], sems["db_recv"], h_src[k])

    def reduce_down(n):
        wait(g_r.at[:, n], sem_g.at[n])
        total = g_f[n, pl.ds(pl.multiple_of(y * R, R), R), :]
        for o in range(3):
            total += g_r[o, n].astype(F32)
        for a in range(2):
            k = 4 * (n % 2) + 2 * a + n // 2
            g_s[k] = total[:, a * B:(a + 1) * B].astype(DOWN_BACK)
            send_any(g_s.at[k], g_own.at[back], sems["gb_send"], sems["gb_recv"], w_src[k])

    for n in range(NC + AHEAD):
        if n < NC:
            multiply_dhid(n)
        if n == PASS_AT:
            pass_hidden()
        if n >= AHEAD:
            reduce_dhid(n - AHEAD)
    wait(three, sems["hg_recv"])
    for n in range(NC + AHEAD):
        if n < NC:
            multiply_down(n)
        if n >= AHEAD:
            reduce_down(n - AHEAD)

    wait(d_own, sems["db_recv"])
    for b in range(FD // 128):
        cols = slice(b * 128, (b + 1) * 128)
        dhid = d_own[cols, :].astype(F32).T
        o_up[:, cols] = (dhid * f_up[:, cols]).astype(BF16)
        o_gate[:, cols] = (dhid * f_gate[:, cols]).astype(BF16)
    wait(g_own, sems["gb_recv"])
    scale = 1.0 / 64.0
    o_down[...] = g_own[...].astype(F32) * scale

    def wait_all(ref, s, count, most):
        for k in (most - 1, most):
            @pl.when(count == k)
            def _():
                wait(ref.at[pl.ds(0, k)], s)

    def wait_rows(ref, s, count):
        for k in (NK - 1, NK):
            @pl.when(count == k)
            def _():
                wait(ref.at[pl.ds(0, k * R)], s)

    for k in (0, 1):
        @pl.when(n_c == len(c_dst) - k)
        def _():
            wait(cot_b.at[0, pl.ds(0, (len(c_dst) - k) // 2 * B)], sems["cot_send"])
            if k:
                wait(cot.at[:, pl.ds(0, B)], sems["cot_send"])
    wait_rows(weight, sems["w_send"], n_w)
    wait_rows(hid_t, sems["h_send"], n_h)

    @pl.when(par == 0)
    def _():
        wait(cot_b.at[pl.ds(0, 2), pl.ds(0, 6 * B)], sems["ring_send_r"])
        wait(cot_b.at[pl.ds(0, 2), pl.ds(0, 5 * B)], sems["ring_send_l"])

    wait(cot_b.at[pl.ds(0, 2)], sems["sib_send"])
    wait(three, sems["wg_send"])
    wait(three, sems["hg_send"])
    wait(d_r, sems["ds_send"])
    wait(g_r, sems["gs_send"])
    wait_all(d_s, sems["db_send"], n_h, NK)
    wait_all(g_s, sems["gb_send"], n_w, NK)


def shards(cotangent, gate_pre, up_pre, down_weight):
    vmem = pl.BlockSpec(memory_space=pltpu.VMEM)
    dma = pltpu.SemaphoreType.DMA
    return pl.pallas_call(
        kernel,
        name="swiglu_down_backward",
        out_shape=(
            jax.ShapeDtypeStruct((B, FD), BF16),
            jax.ShapeDtypeStruct((B, FD), BF16),
            jax.ShapeDtypeStruct((FD, B), F32),
        ),
        in_specs=[pl.BlockSpec(memory_space=pltpu.HBM)] * 4,
        out_specs=(vmem,) * 3,
        scratch_shapes=[
            pltpu.VMEM((B, 2 * B), BF16),
            pltpu.VMEM((B, FD), BF16),
            pltpu.VMEM((B, FD), BF16),
            pltpu.VMEM((FD, B), BF16),
            pltpu.VMEM((FD, B), BF16),
            pltpu.VMEM((B, FD), F32),
            pltpu.VMEM((B, FD), F32),
            pltpu.VMEM((NC, NK * B, CH), BF16),
            pltpu.VMEM((NC, RS, CH), BF16),
            pltpu.VMEM((NC, RS, CH), BF16),
            pltpu.VMEM((NC, RS, CH), F32),
            pltpu.VMEM((NX, NC, R, CH), GRAD_SUM),
            pltpu.VMEM((3, NC, R, CH), GRAD_SUM),
            pltpu.VMEM((NK, R, B), GRAD_BACK),
            pltpu.VMEM((FD, B), GRAD_BACK),
            pltpu.VMEM((NC, RS, CH), F32),
            pltpu.VMEM((NX, NC, R, CH), DOWN_SUM),
            pltpu.VMEM((3, NC, R, CH), DOWN_SUM),
            pltpu.VMEM((NK, R, B), DOWN_BACK),
            pltpu.VMEM((FD, B), DOWN_BACK),
            dma((5,)), dma((9 * NP,)), dma((8 * NP,)), dma((NK,)), dma((NK,)), dma((NC,)), dma((NC,)), dma((4,)), dma((17,)),
        ],
        compiler_params=pltpu.CompilerParams(
            collective_id=0, has_side_effects=True, vmem_limit_bytes=60 * 2**20),
        cost_estimate=pl.CostEstimate(flops=4 * RS * 1024 * 1024, bytes_accessed=2 * 2**20, transcendentals=B * FD),
    )(cotangent, gate_pre, up_pre, down_weight)


def solution(mesh):
    in_specs = (P("dp", "tensor"), P("dp", "tensor"), P("dp", "tensor"), P("tensor", "dp"))
    out_specs = (P("dp", "tensor"), P("dp", "tensor"), P("tensor", "dp"))
    return jax.shard_map(shards, mesh=mesh, in_specs=in_specs, out_specs=out_specs, check_vma=False)
```

```python
import jax
import jax.numpy as jnp
from jax import lax
from jax.experimental import pallas as pl
from jax.experimental.pallas import tpu as pltpu
from jax.sharding import PartitionSpec as P

MESH = pl.DeviceIdType.MESH
F32, BF16 = jnp.float32, jnp.bfloat16
NX, NZ = 4, 16
NK = NZ // 2
B = 128
FD = 896
R = FD // NK
RS = NX * R
NC, CH = 4, 256

NP, PR = 2, B // 2

AHEAD = 2
ALL = range(NK)
PLAN = ([("w", ALL), ("h", ALL)], [], ["pass_w", "pass_h"], [], [])

GRAD_SUM = BF16
GRAD_BACK = F32
DOWN_SUM = BF16
DOWN_BACK = BF16


def kernel(cot_in, gate_in, up_in, weight_in, o_gate, o_up, o_down,
           cot, gate, up, weight, hid_t, f_up, f_gate, cot_b, w_g, h_g,
           d_f, d_p, d_r, d_s, d_own,
           g_f, g_p, g_r, g_s, g_own,
           sem_near, sem_ring_r, sem_ring_l, sem_w, sem_h, sem_d, sem_g, sem_in, sem):
    i, j = lax.axis_index("dp"), lax.axis_index("tensor")
    yh, z = i // NZ, i % NZ
    x, yl, c = j // 4, (j // 2) % 2, j % 2
    y = yh * 2 + yl
    par = (z + yl) % 2
    me = i * 16 + j

    def dev(x, yh, yl, z, c):
        return yh * NZ + z, x * 4 + yl * 2 + c

    def is_me(d):
        return d[0] * 16 + d[1] == me

    names = ["cot_send", "w_send", "h_send", "ring_send_r", "ring_send_l",
             "sib_send", "sib_recv", "wg_send", "wg_recv", "hg_send", "hg_recv", "ds_send", "gs_send",
             "db_send", "db_recv", "gb_send", "gb_recv"]
    sems = {n: sem.at[k] for k, n in enumerate(names)}

    def remote(src, dst, send, recv, d):
        return pltpu.make_async_remote_copy(
            src_ref=src, dst_ref=dst, send_sem=send, recv_sem=recv, device_id=d, device_id_type=MESH)

    def send_any(src, dst, send, recv, d):
        @pl.when(is_me(d))
        def _():
            pltpu.make_async_copy(src, dst, recv).start()

        @pl.when(jnp.logical_not(is_me(d)))
        def _():
            remote(src, dst, send, recv, d).start()

    def wait(ref, s):
        pltpu.make_async_copy(ref, ref, s).wait()

    h_dst = [dev(x, yh, z % 2, 2 * s + c, yl) for s in range(NK)]
    w_dst = [dev(2 * yh + z % 2, x // 2, x % 2, 2 * s + c, yl) for s in range(NK)]
    near = (0, 1, -1, 2, -2)
    c_dst = [(o, e, dev(2 * (x // 2) + e, yh, z % 2, (z + o + NZ) % NZ, c)) for o in near for e in range(2)]
    h_src = [dev(x, yh, c, 2 * k + yl, z % 2) for k in range(NK)]
    w_src = [dev(y, x // 2, c, 2 * k + x % 2, z % 2) for k in range(NK)]
    c_src = [(abs(o) % 2, dev(2 * (x // 2) + a, yh, b, (z + o + NZ) % NZ, c))
             for o in near for a in range(2) for b in range(2)]
    right, left = dev(x, yh, yl, (z + 1) % NZ, c), dev(x, yh, yl, (z + NZ - 1) % NZ, c)
    right2, left2 = dev(x, yh, yl, (z + 2) % NZ, c), dev(x, yh, yl, (z + NZ - 2) % NZ, c)
    sibling = dev(x, yh, yl, z, 1 - c)
    x_dst = [dev((x + o) % 4, yh, yl, z, c) for o in range(1, 4)]
    y_idx = [(y + o) % 4 for o in range(1, 4)]
    y_dst = [dev(x, v // 2, v % 2, z, c) for v in y_idx]

    loads = [pltpu.make_async_copy(a, b, sem_in.at[k])
             for k, (a, b) in enumerate([(gate_in, gate), (up_in, up), (cot_in, cot), (weight_in, weight)])]
    for load in loads:
        load.start()

    barrier = pltpu.get_barrier_semaphore()

    def greet(d):
        pl.semaphore_signal(barrier, inc=1, device_id=d, device_id_type=MESH)

    for d in h_src + w_src:
        @pl.when(jnp.logical_not(is_me(d)))
        def _():
            greet(d)
    for odd, d in c_src:
        @pl.when(jnp.logical_and(par == odd, jnp.logical_not(is_me(d))))
        def _():
            greet(d)
    for d in [right, left, right2, left2, sibling] + x_dst + y_dst:
        greet(d)

    loads[0].wait()
    loads[1].wait()
    for b in range(FD // 128):
        cols = slice(b * 128, (b + 1) * 128)
        g, u = gate[:, cols].astype(F32), up[:, cols].astype(F32)
        sig = jax.nn.sigmoid(g)
        act = g * sig
        hid_t[cols, :] = (act * u).T.astype(BF16)

    def others(dsts):
        n = jnp.int32(0)
        for d in dsts:
            n = n + jnp.where(is_me(d), 0, 1)
        return n

    loads[2].wait()
    loads[3].wait()
    n_h, n_w, n_c = others(h_dst), others(w_dst), others([d for _, _, d in c_dst])
    pl.semaphore_wait(barrier, n_h + n_w + n_c + 11)

    kz = z // 2

    def send_cot():
        for o, e, d in c_dst:
            send_any(cot.at[:, pl.ds(e * B, B)],
                     cot_b.at[c * 2 + x % 2, pl.ds((z // 2) * B, B), pl.ds(yl * B, B)],
                     sems["cot_send"], sem_near.at[o + 2], d)

    def send_weights(part):
        for s in part:
            send_any(weight.at[pl.ds(s * R, R)],
                     w_g.at[(kz % 2) * 2 + kz // 4, pl.ds(x * R, R), pl.ds(((kz // 2) % 2) * B, B)],
                     sems["w_send"], sem_w.at[kz], w_dst[s])

    send_cot()

    def send_hidden(part):
        for s in part:
            send_any(hid_t.at[pl.ds(s * R, R)],
                     h_g.at[kz // 2, pl.ds(x * R, R), pl.ds((kz % 2) * B, B)],
                     sems["h_send"], sem_h.at[kz], h_dst[s])

    for b in range(FD // 128):
        cols = slice(b * 128, (b + 1) * 128)
        g, u = gate[:, cols].astype(F32), up[:, cols].astype(F32)
        sig = jax.nn.sigmoid(g)
        f_up[:, cols] = g * sig
        f_gate[:, cols] = u * sig * (1.0 + g * (1.0 - sig))

    def panel(zt):
        return cot_b.at[pl.ds(2 * c, 2), pl.ds(((zt + 2 * NZ) % NZ) // 2 * B, B)]

    def forward(ref, d, send, recv):
        remote(ref, ref, send, recv, d).start()

    def piece(zt, q):
        return cot_b.at[pl.ds(2 * c, 2), pl.ds(((zt + 2 * NZ) % NZ) // 2 * B + q * PR, PR)]

    three = h_g.at[:, pl.ds(0, 3 * R)]

    def pass_weights():
        for q in range(NC):
            mine = w_g.at[q, pl.ds(y * R, R)]
            for a in range(2):
                wait(mine.at[:, pl.ds(a * B, B)], sem_w.at[(q % 2) * 4 + 2 * a + q // 2])
            for d in y_dst:
                forward(mine, d, sems["wg_send"], sems["wg_recv"])

    def pass_hidden():
        for q in range(NC):
            mine = h_g.at[q, pl.ds(x * R, R)]
            for a in range(2):
                wait(mine.at[:, pl.ds(a * B, B)], sem_h.at[2 * q + a])
            for d in x_dst:
                forward(mine, d, sems["hg_send"], sems["hg_recv"])

    def to_sibling(zt):
        forward(panel(zt), sibling, sems["sib_send"], sems["sib_recv"])

    def act(point):
        for what in PLAN[point]:
            if what == "pass_w":
                pass_weights()
            elif what == "pass_h":
                pass_hidden()
            else:
                (send_weights if what[0] == "w" else send_hidden)(what[1])

    act(0)

    def hand_on(zt, d, q, one, two, send, recv):
        forward(piece(zt, q), two, send, recv.at[(d + 2) * NP + q]) if two is not None else None
        forward(piece(zt, q), one, send, recv.at[(d + 1) * NP + q])

    for t in range(4):
        @pl.when(par == 0)
        def _():
            d = 2 * t + 2
            if t == 0:
                wait(panel(z - 2), sem_near.at[4])
                wait(panel(z + 2), sem_near.at[0])
            for q in range(NP):
                if t > 0:
                    wait(piece(z - d, q), sem_ring_r.at[d * NP + q])
                if t < 3:
                    hand_on(z - d, d, q, right, right2, sems["ring_send_r"], sem_ring_r)
                    if t > 0:
                        wait(piece(z + d, q), sem_ring_l.at[d * NP + q])
                    hand_on(z + d, d, q, left, left2 if t < 2 else None, sems["ring_send_l"], sem_ring_l)
            to_sibling(z - d)
            if t < 3:
                to_sibling(z + d)
            if t == 0:
                wait(panel(z), sem_near.at[2])
                to_sibling(z)

        @pl.when(par == 1)
        def _():
            d = 2 * t + 1
            if t == 0:
                wait(panel(z - 1), sem_near.at[3])
                wait(panel(z + 1), sem_near.at[1])
            else:
                for q in range(NP):
                    wait(piece(z - d, q), sem_ring_r.at[d * NP + q])
                    wait(piece(z + d, q), sem_ring_l.at[d * NP + q])
            to_sibling(z - d)
            to_sibling(z + d)

        act(t + 1)

    wait(cot_b.at[pl.ds(2 * (1 - c), 2)], sems["sib_recv"])
    wait(three, sems["wg_recv"])

    def multiply_dhid(n):
        total = jnp.zeros((RS, CH), F32)
        for q in range(NC):
            total += lax.dot_general(w_g[q], cot_b[q, n * CH:(n + 1) * CH, :], (((1,), (1,)), ((), ())),
                                     preferred_element_type=F32)
        d_f[n] = total
        for v in range(NX):
            d_p[v, n] = total[v * R:(v + 1) * R].astype(GRAD_SUM)
        for o in range(1, 4):
            remote(d_p.at[(x + o) % 4, n], d_r.at[o - 1, n], sems["ds_send"], sem_d.at[n], x_dst[o - 1]).start()

    def multiply_down(n):
        total = jnp.zeros((RS, CH), F32)
        for q in range(NC):
            total += jnp.dot(h_g[q], cot_b[n, q * CH:(q + 1) * CH, :], preferred_element_type=F32)
        g_f[n] = total
        for v in range(NX):
            g_p[v, n] = total[v * R:(v + 1) * R].astype(DOWN_SUM)
        for o in range(1, 4):
            remote(g_p.at[y_idx[o - 1], n], g_r.at[o - 1, n], sems["gs_send"], sem_g.at[n], y_dst[o - 1]).start()

    back = pl.ds(pl.multiple_of((z // 2) * R, R), R)

    def reduce_dhid(n):
        wait(d_r.at[:, n], sem_d.at[n])
        total = d_f[n, pl.ds(pl.multiple_of(x * R, R), R), :]
        for o in range(3):
            total += d_r[o, n].astype(F32)
        for a in range(2):
            k = 2 * n + a
            d_s[k] = total[:, a * B:(a + 1) * B].astype(GRAD_BACK)
            send_any(d_s.at[k], d_own.at[back], sems["db_send"], sems["db_recv"], h_src[k])

    def reduce_down(n):
        wait(g_r.at[:, n], sem_g.at[n])
        total = g_f[n, pl.ds(pl.multiple_of(y * R, R), R), :]
        for o in range(3):
            total += g_r[o, n].astype(F32)
        for a in range(2):
            k = 4 * (n % 2) + 2 * a + n // 2
            g_s[k] = total[:, a * B:(a + 1) * B].astype(DOWN_BACK)
            send_any(g_s.at[k], g_own.at[back], sems["gb_send"], sems["gb_recv"], w_src[k])

    wait(three, sems["hg_recv"])
    for n in range(NC + AHEAD):
        if n < NC:
            multiply_dhid(n)
            multiply_down(n)
        if n >= AHEAD:
            reduce_dhid(n - AHEAD)
            reduce_down(n - AHEAD)

    wait(d_own, sems["db_recv"])
    for b in range(FD // 128):
        cols = slice(b * 128, (b + 1) * 128)
        dhid = d_own[cols, :].astype(F32).T
        o_up[:, cols] = (dhid * f_up[:, cols]).astype(BF16)
        o_gate[:, cols] = (dhid * f_gate[:, cols]).astype(BF16)
    wait(g_own, sems["gb_recv"])
    scale = 1.0 / 64.0
    o_down[...] = g_own[...].astype(F32) * scale

    def wait_all(ref, s, count, most):
        for k in (most - 1, most):
            @pl.when(count == k)
            def _():
                wait(ref.at[pl.ds(0, k)], s)

    def wait_rows(ref, s, count):
        for k in (NK - 1, NK):
            @pl.when(count == k)
            def _():
                wait(ref.at[pl.ds(0, k * R)], s)

    for k in (0, 1):
        @pl.when(n_c == len(c_dst) - k)
        def _():
            wait(cot_b.at[0, pl.ds(0, (len(c_dst) - k) // 2 * B)], sems["cot_send"])
            if k:
                wait(cot.at[:, pl.ds(0, B)], sems["cot_send"])
    wait_rows(weight, sems["w_send"], n_w)
    wait_rows(hid_t, sems["h_send"], n_h)

    @pl.when(par == 0)
    def _():
        wait(cot_b.at[pl.ds(0, 2), pl.ds(0, 6 * B)], sems["ring_send_r"])
        wait(cot_b.at[pl.ds(0, 2), pl.ds(0, 5 * B)], sems["ring_send_l"])

    wait(cot_b.at[pl.ds(0, 2)], sems["sib_send"])
    wait(three, sems["wg_send"])
    wait(three, sems["hg_send"])
    wait(d_r, sems["ds_send"])
    wait(g_r, sems["gs_send"])
    wait_all(d_s, sems["db_send"], n_h, NK)
    wait_all(g_s, sems["gb_send"], n_w, NK)


def shards(cotangent, gate_pre, up_pre, down_weight):
    vmem = pl.BlockSpec(memory_space=pltpu.VMEM)
    dma = pltpu.SemaphoreType.DMA
    return pl.pallas_call(
        kernel,
        name="swiglu_down_backward",
        out_shape=(
            jax.ShapeDtypeStruct((B, FD), BF16),
            jax.ShapeDtypeStruct((B, FD), BF16),
            jax.ShapeDtypeStruct((FD, B), F32),
        ),
        in_specs=[pl.BlockSpec(memory_space=pltpu.HBM)] * 4,
        out_specs=(vmem,) * 3,
        scratch_shapes=[
            pltpu.VMEM((B, 2 * B), BF16),
            pltpu.VMEM((B, FD), BF16),
            pltpu.VMEM((B, FD), BF16),
            pltpu.VMEM((FD, B), BF16),
            pltpu.VMEM((FD, B), BF16),
            pltpu.VMEM((B, FD), F32),
            pltpu.VMEM((B, FD), F32),
            pltpu.VMEM((NC, NK * B, CH), BF16),
            pltpu.VMEM((NC, RS, CH), BF16),
            pltpu.VMEM((NC, RS, CH), BF16),
            pltpu.VMEM((NC, RS, CH), F32),
            pltpu.VMEM((NX, NC, R, CH), GRAD_SUM),
            pltpu.VMEM((3, NC, R, CH), GRAD_SUM),
            pltpu.VMEM((NK, R, B), GRAD_BACK),
            pltpu.VMEM((FD, B), GRAD_BACK),
            pltpu.VMEM((NC, RS, CH), F32),
            pltpu.VMEM((NX, NC, R, CH), DOWN_SUM),
            pltpu.VMEM((3, NC, R, CH), DOWN_SUM),
            pltpu.VMEM((NK, R, B), DOWN_BACK),
            pltpu.VMEM((FD, B), DOWN_BACK),
            dma((5,)), dma((9 * NP,)), dma((8 * NP,)), dma((NK,)), dma((NK,)), dma((NC,)), dma((NC,)), dma((4,)), dma((17,)),
        ],
        compiler_params=pltpu.CompilerParams(
            collective_id=0, has_side_effects=True, vmem_limit_bytes=60 * 2**20),
        cost_estimate=pl.CostEstimate(flops=4 * RS * 1024 * 1024, bytes_accessed=2 * 2**20, transcendentals=B * FD),
    )(cotangent, gate_pre, up_pre, down_weight)


def solution(mesh):
    in_specs = (P("dp", "tensor"), P("dp", "tensor"), P("dp", "tensor"), P("tensor", "dp"))
    out_specs = (P("dp", "tensor"), P("dp", "tensor"), P("tensor", "dp"))
    return jax.shard_map(shards, mesh=mesh, in_specs=in_specs, out_specs=out_specs, check_vma=False)
```

```python
import jax
import jax.numpy as jnp
from jax import lax
from jax.experimental import pallas as pl
from jax.experimental.pallas import tpu as pltpu
from jax.sharding import PartitionSpec as P

MESH = pl.DeviceIdType.MESH
F32, BF16 = jnp.float32, jnp.bfloat16
NX, NZ = 4, 16
NK = NZ // 2
B = 128
FD = 896
R = FD // NK
RS = NX * R
NC, CH = 4, 256

NP, PR = 2, B // 2

AHEAD = 2
ALL = range(NK)
PLAN = ([("w", ALL), ("h", ALL)], ["pass_w"], ["pass_h"], [], [])

GRAD_SUM = BF16
GRAD_BACK = F32
DOWN_SUM = BF16
DOWN_BACK = BF16


def kernel(cot_in, gate_in, up_in, weight_in, o_gate, o_up, o_down,
           cot, gate, up, weight, hid_t, f_up, f_gate, cot_b, w_g, h_g,
           d_f, d_p, d_r, d_s, d_own,
           g_f, g_p, g_r, g_s, g_own,
           sem_near, sem_ring_r, sem_ring_l, sem_w, sem_h, sem_d, sem_g, sem_in, sem):
    i, j = lax.axis_index("dp"), lax.axis_index("tensor")
    yh, z = i // NZ, i % NZ
    x, yl, c = j // 4, (j // 2) % 2, j % 2
    y = yh * 2 + yl
    par = (z + yl) % 2
    me = i * 16 + j

    def dev(x, yh, yl, z, c):
        return yh * NZ + z, x * 4 + yl * 2 + c

    def is_me(d):
        return d[0] * 16 + d[1] == me

    names = ["cot_send", "w_send", "h_send", "ring_send_r", "ring_send_l",
             "sib_send", "sib_recv", "wg_send", "wg_recv", "hg_send", "hg_recv", "ds_send", "gs_send",
             "db_send", "db_recv", "gb_send", "gb_recv"]
    sems = {n: sem.at[k] for k, n in enumerate(names)}

    def remote(src, dst, send, recv, d):
        return pltpu.make_async_remote_copy(
            src_ref=src, dst_ref=dst, send_sem=send, recv_sem=recv, device_id=d, device_id_type=MESH)

    def send_any(src, dst, send, recv, d):
        @pl.when(is_me(d))
        def _():
            pltpu.make_async_copy(src, dst, recv).start()

        @pl.when(jnp.logical_not(is_me(d)))
        def _():
            remote(src, dst, send, recv, d).start()

    def wait(ref, s):
        pltpu.make_async_copy(ref, ref, s).wait()

    h_dst = [dev(x, yh, z % 2, 2 * s + c, yl) for s in range(NK)]
    w_dst = [dev(2 * yh + z % 2, x // 2, x % 2, 2 * s + c, yl) for s in range(NK)]
    near = (0, 1, -1, 2, -2)
    c_dst = [(o, e, dev(2 * (x // 2) + e, yh, z % 2, (z + o + NZ) % NZ, c)) for o in near for e in range(2)]
    h_src = [dev(x, yh, c, 2 * k + yl, z % 2) for k in range(NK)]
    w_src = [dev(y, x // 2, c, 2 * k + x % 2, z % 2) for k in range(NK)]
    c_src = [(abs(o) % 2, dev(2 * (x // 2) + a, yh, b, (z + o + NZ) % NZ, c))
             for o in near for a in range(2) for b in range(2)]
    right, left = dev(x, yh, yl, (z + 1) % NZ, c), dev(x, yh, yl, (z + NZ - 1) % NZ, c)
    right2, left2 = dev(x, yh, yl, (z + 2) % NZ, c), dev(x, yh, yl, (z + NZ - 2) % NZ, c)
    sibling = dev(x, yh, yl, z, 1 - c)
    x_dst = [dev((x + o) % 4, yh, yl, z, c) for o in range(1, 4)]
    y_idx = [(y + o) % 4 for o in range(1, 4)]
    y_dst = [dev(x, v // 2, v % 2, z, c) for v in y_idx]

    loads = [pltpu.make_async_copy(a, b, sem_in.at[k])
             for k, (a, b) in enumerate([(gate_in, gate), (up_in, up), (cot_in, cot), (weight_in, weight)])]
    for load in loads:
        load.start()

    barrier = pltpu.get_barrier_semaphore()

    def greet(d):
        pl.semaphore_signal(barrier, inc=1, device_id=d, device_id_type=MESH)

    for d in h_src + w_src:
        @pl.when(jnp.logical_not(is_me(d)))
        def _():
            greet(d)
    for odd, d in c_src:
        @pl.when(jnp.logical_and(par == odd, jnp.logical_not(is_me(d))))
        def _():
            greet(d)
    for d in [right, left, right2, left2, sibling] + x_dst + y_dst:
        greet(d)

    loads[0].wait()
    loads[1].wait()
    for b in range(FD // 128):
        cols = slice(b * 128, (b + 1) * 128)
        g, u = gate[:, cols].astype(F32), up[:, cols].astype(F32)
        sig = jax.nn.sigmoid(g)
        act = g * sig
        hid_t[cols, :] = (act * u).T.astype(BF16)

    def others(dsts):
        n = jnp.int32(0)
        for d in dsts:
            n = n + jnp.where(is_me(d), 0, 1)
        return n

    loads[2].wait()
    loads[3].wait()
    n_h, n_w, n_c = others(h_dst), others(w_dst), others([d for _, _, d in c_dst])
    pl.semaphore_wait(barrier, n_h + n_w + n_c + 11)

    kz = z // 2

    def send_cot():
        for o, e, d in c_dst:
            send_any(cot.at[:, pl.ds(e * B, B)],
                     cot_b.at[c * 2 + x % 2, pl.ds((z // 2) * B, B), pl.ds(yl * B, B)],
                     sems["cot_send"], sem_near.at[o + 2], d)

    def send_weights(part):
        for s in part:
            send_any(weight.at[pl.ds(s * R, R)],
                     w_g.at[(kz % 2) * 2 + kz // 4, pl.ds(x * R, R), pl.ds(((kz // 2) % 2) * B, B)],
                     sems["w_send"], sem_w.at[kz], w_dst[s])

    send_cot()

    def send_hidden(part):
        for s in part:
            send_any(hid_t.at[pl.ds(s * R, R)],
                     h_g.at[kz // 2, pl.ds(x * R, R), pl.ds((kz % 2) * B, B)],
                     sems["h_send"], sem_h.at[kz], h_dst[s])

    for b in range(FD // 128):
        cols = slice(b * 128, (b + 1) * 128)
        g, u = gate[:, cols].astype(F32), up[:, cols].astype(F32)
        sig = jax.nn.sigmoid(g)
        f_up[:, cols] = g * sig
        f_gate[:, cols] = u * sig * (1.0 + g * (1.0 - sig))

    def panel(zt):
        return cot_b.at[pl.ds(2 * c, 2), pl.ds(((zt + 2 * NZ) % NZ) // 2 * B, B)]

    def forward(ref, d, send, recv):
        remote(ref, ref, send, recv, d).start()

    def piece(zt, q):
        return cot_b.at[pl.ds(2 * c, 2), pl.ds(((zt + 2 * NZ) % NZ) // 2 * B + q * PR, PR)]

    three = h_g.at[:, pl.ds(0, 3 * R)]

    def pass_weights():
        for q in range(NC):
            mine = w_g.at[q, pl.ds(y * R, R)]
            for a in range(2):
                wait(mine.at[:, pl.ds(a * B, B)], sem_w.at[(q % 2) * 4 + 2 * a + q // 2])
            for d in y_dst:
                forward(mine, d, sems["wg_send"], sems["wg_recv"])

    def pass_hidden():
        for q in range(NC):
            mine = h_g.at[q, pl.ds(x * R, R)]
            for a in range(2):
                wait(mine.at[:, pl.ds(a * B, B)], sem_h.at[2 * q + a])
            for d in x_dst:
                forward(mine, d, sems["hg_send"], sems["hg_recv"])

    def to_sibling(zt):
        forward(panel(zt), sibling, sems["sib_send"], sems["sib_recv"])

    def act(point):
        for what in PLAN[point]:
            if what == "pass_w":
                pass_weights()
            elif what == "pass_h":
                pass_hidden()
            else:
                (send_weights if what[0] == "w" else send_hidden)(what[1])

    act(0)

    def hand_on(zt, d, q, one, two, send, recv):
        forward(piece(zt, q), two, send, recv.at[(d + 2) * NP + q]) if two is not None else None
        forward(piece(zt, q), one, send, recv.at[(d + 1) * NP + q])

    for t in range(4):
        @pl.when(par == 0)
        def _():
            d = 2 * t + 2
            if t == 0:
                wait(panel(z - 2), sem_near.at[4])
                wait(panel(z + 2), sem_near.at[0])
            for q in range(NP):
                if t > 0:
                    wait(piece(z - d, q), sem_ring_r.at[d * NP + q])
                if t < 3:
                    hand_on(z - d, d, q, right, right2, sems["ring_send_r"], sem_ring_r)
                    if t > 0:
                        wait(piece(z + d, q), sem_ring_l.at[d * NP + q])
                    hand_on(z + d, d, q, left, left2 if t < 2 else None, sems["ring_send_l"], sem_ring_l)
            to_sibling(z - d)
            if t < 3:
                to_sibling(z + d)
            if t == 0:
                wait(panel(z), sem_near.at[2])
                to_sibling(z)

        @pl.when(par == 1)
        def _():
            d = 2 * t + 1
            if t == 0:
                wait(panel(z - 1), sem_near.at[3])
                wait(panel(z + 1), sem_near.at[1])
            else:
                for q in range(NP):
                    wait(piece(z - d, q), sem_ring_r.at[d * NP + q])
                    wait(piece(z + d, q), sem_ring_l.at[d * NP + q])
            to_sibling(z - d)
            to_sibling(z + d)

        act(t + 1)

    wait(cot_b.at[pl.ds(2 * (1 - c), 2)], sems["sib_recv"])
    wait(three, sems["wg_recv"])

    def multiply_dhid(n):
        total = jnp.zeros((RS, CH), F32)
        for q in range(NC):
            total += lax.dot_general(w_g[q], cot_b[q, n * CH:(n + 1) * CH, :], (((1,), (1,)), ((), ())),
                                     preferred_element_type=F32)
        d_f[n] = total
        for v in range(NX):
            d_p[v, n] = total[v * R:(v + 1) * R].astype(GRAD_SUM)
        for o in range(1, 4):
            remote(d_p.at[(x + o) % 4, n], d_r.at[o - 1, n], sems["ds_send"], sem_d.at[n], x_dst[o - 1]).start()

    def multiply_down(n):
        total = jnp.zeros((RS, CH), F32)
        for q in range(NC):
            total += jnp.dot(h_g[q], cot_b[n, q * CH:(q + 1) * CH, :], preferred_element_type=F32)
        g_f[n] = total
        for v in range(NX):
            g_p[v, n] = total[v * R:(v + 1) * R].astype(DOWN_SUM)
        for o in range(1, 4):
            remote(g_p.at[y_idx[o - 1], n], g_r.at[o - 1, n], sems["gs_send"], sem_g.at[n], y_dst[o - 1]).start()

    back = pl.ds(pl.multiple_of((z // 2) * R, R), R)

    def reduce_dhid(n):
        wait(d_r.at[:, n], sem_d.at[n])
        total = d_f[n, pl.ds(pl.multiple_of(x * R, R), R), :]
        for o in range(3):
            total += d_r[o, n].astype(F32)
        for a in range(2):
            k = 2 * n + a
            d_s[k] = total[:, a * B:(a + 1) * B].astype(GRAD_BACK)
            send_any(d_s.at[k], d_own.at[back], sems["db_send"], sems["db_recv"], h_src[k])

    def reduce_down(n):
        wait(g_r.at[:, n], sem_g.at[n])
        total = g_f[n, pl.ds(pl.multiple_of(y * R, R), R), :]
        for o in range(3):
            total += g_r[o, n].astype(F32)
        for a in range(2):
            k = 4 * (n % 2) + 2 * a + n // 2
            g_s[k] = total[:, a * B:(a + 1) * B].astype(DOWN_BACK)
            send_any(g_s.at[k], g_own.at[back], sems["gb_send"], sems["gb_recv"], w_src[k])

    wait(three, sems["hg_recv"])
    for n in range(NC + AHEAD):
        if n < NC:
            multiply_dhid(n)
            multiply_down(n)
        if n >= AHEAD:
            reduce_dhid(n - AHEAD)
            reduce_down(n - AHEAD)

    wait(d_own, sems["db_recv"])
    for b in range(FD // 128):
        cols = slice(b * 128, (b + 1) * 128)
        dhid = d_own[cols, :].astype(F32).T
        o_up[:, cols] = (dhid * f_up[:, cols]).astype(BF16)
        o_gate[:, cols] = (dhid * f_gate[:, cols]).astype(BF16)
    wait(g_own, sems["gb_recv"])
    scale = 1.0 / 64.0
    o_down[...] = g_own[...].astype(F32) * scale

    def wait_all(ref, s, count, most):
        for k in (most - 1, most):
            @pl.when(count == k)
            def _():
                wait(ref.at[pl.ds(0, k)], s)

    def wait_rows(ref, s, count):
        for k in (NK - 1, NK):
            @pl.when(count == k)
            def _():
                wait(ref.at[pl.ds(0, k * R)], s)

    for k in (0, 1):
        @pl.when(n_c == len(c_dst) - k)
        def _():
            wait(cot_b.at[0, pl.ds(0, (len(c_dst) - k) // 2 * B)], sems["cot_send"])
            if k:
                wait(cot.at[:, pl.ds(0, B)], sems["cot_send"])
    wait_rows(weight, sems["w_send"], n_w)
    wait_rows(hid_t, sems["h_send"], n_h)

    @pl.when(par == 0)
    def _():
        wait(cot_b.at[pl.ds(0, 2), pl.ds(0, 6 * B)], sems["ring_send_r"])
        wait(cot_b.at[pl.ds(0, 2), pl.ds(0, 5 * B)], sems["ring_send_l"])

    wait(cot_b.at[pl.ds(0, 2)], sems["sib_send"])
    wait(three, sems["wg_send"])
    wait(three, sems["hg_send"])
    wait(d_r, sems["ds_send"])
    wait(g_r, sems["gs_send"])
    wait_all(d_s, sems["db_send"], n_h, NK)
    wait_all(g_s, sems["gb_send"], n_w, NK)


def shards(cotangent, gate_pre, up_pre, down_weight):
    vmem = pl.BlockSpec(memory_space=pltpu.VMEM)
    dma = pltpu.SemaphoreType.DMA
    return pl.pallas_call(
        kernel,
        name="swiglu_down_backward",
        out_shape=(
            jax.ShapeDtypeStruct((B, FD), BF16),
            jax.ShapeDtypeStruct((B, FD), BF16),
            jax.ShapeDtypeStruct((FD, B), F32),
        ),
        in_specs=[pl.BlockSpec(memory_space=pltpu.HBM)] * 4,
        out_specs=(vmem,) * 3,
        scratch_shapes=[
            pltpu.VMEM((B, 2 * B), BF16),
            pltpu.VMEM((B, FD), BF16),
            pltpu.VMEM((B, FD), BF16),
            pltpu.VMEM((FD, B), BF16),
            pltpu.VMEM((FD, B), BF16),
            pltpu.VMEM((B, FD), F32),
            pltpu.VMEM((B, FD), F32),
            pltpu.VMEM((NC, NK * B, CH), BF16),
            pltpu.VMEM((NC, RS, CH), BF16),
            pltpu.VMEM((NC, RS, CH), BF16),
            pltpu.VMEM((NC, RS, CH), F32),
            pltpu.VMEM((NX, NC, R, CH), GRAD_SUM),
            pltpu.VMEM((3, NC, R, CH), GRAD_SUM),
            pltpu.VMEM((NK, R, B), GRAD_BACK),
            pltpu.VMEM((FD, B), GRAD_BACK),
            pltpu.VMEM((NC, RS, CH), F32),
            pltpu.VMEM((NX, NC, R, CH), DOWN_SUM),
            pltpu.VMEM((3, NC, R, CH), DOWN_SUM),
            pltpu.VMEM((NK, R, B), DOWN_BACK),
            pltpu.VMEM((FD, B), DOWN_BACK),
            dma((5,)), dma((9 * NP,)), dma((8 * NP,)), dma((NK,)), dma((NK,)), dma((NC,)), dma((NC,)), dma((4,)), dma((17,)),
        ],
        compiler_params=pltpu.CompilerParams(
            collective_id=0, has_side_effects=True, vmem_limit_bytes=60 * 2**20),
        cost_estimate=pl.CostEstimate(flops=4 * RS * 1024 * 1024, bytes_accessed=2 * 2**20, transcendentals=B * FD),
    )(cotangent, gate_pre, up_pre, down_weight)


def solution(mesh):
    in_specs = (P("dp", "tensor"), P("dp", "tensor"), P("dp", "tensor"), P("tensor", "dp"))
    out_specs = (P("dp", "tensor"), P("dp", "tensor"), P("tensor", "dp"))
    return jax.shard_map(shards, mesh=mesh, in_specs=in_specs, out_specs=out_specs, check_vma=False)
```

```python
import jax
import jax.numpy as jnp
from jax import lax
from jax.experimental import pallas as pl
from jax.experimental.pallas import tpu as pltpu
from jax.sharding import PartitionSpec as P

MESH = pl.DeviceIdType.MESH
F32, BF16 = jnp.float32, jnp.bfloat16
NX, NZ = 4, 16
NK = NZ // 2
B = 128
FD = 896
R = FD // NK
RS = NX * R
NC, CH = 4, 256

NP, PR = 2, B // 2

AHEAD = 2
ALL = range(NK)
PLAN = ([("w", ALL), ("h", ALL)], ["pass_w", "pass_h"], [], [], [])

GRAD_SUM = BF16
GRAD_BACK = F32
DOWN_SUM = BF16
DOWN_BACK = BF16


def kernel(cot_in, gate_in, up_in, weight_in, o_gate, o_up, o_down,
           cot, gate, up, weight, hid_t, f_up, f_gate, cot_b, w_g, h_g,
           d_f, d_p, d_r, d_s, d_own,
           g_f, g_p, g_r, g_s, g_own,
           sem_near, sem_ring_r, sem_ring_l, sem_w, sem_h, sem_d, sem_g, sem_in, sem):
    i, j = lax.axis_index("dp"), lax.axis_index("tensor")
    yh, z = i // NZ, i % NZ
    x, yl, c = j // 4, (j // 2) % 2, j % 2
    y = yh * 2 + yl
    par = (z + yl) % 2
    me = i * 16 + j

    def dev(x, yh, yl, z, c):
        return yh * NZ + z, x * 4 + yl * 2 + c

    def is_me(d):
        return d[0] * 16 + d[1] == me

    names = ["cot_send", "w_send", "h_send", "ring_send_r", "ring_send_l",
             "sib_send", "sib_recv", "wg_send", "wg_recv", "hg_send", "hg_recv", "ds_send", "gs_send",
             "db_send", "db_recv", "gb_send", "gb_recv"]
    sems = {n: sem.at[k] for k, n in enumerate(names)}

    def remote(src, dst, send, recv, d):
        return pltpu.make_async_remote_copy(
            src_ref=src, dst_ref=dst, send_sem=send, recv_sem=recv, device_id=d, device_id_type=MESH)

    def send_any(src, dst, send, recv, d):
        @pl.when(is_me(d))
        def _():
            pltpu.make_async_copy(src, dst, recv).start()

        @pl.when(jnp.logical_not(is_me(d)))
        def _():
            remote(src, dst, send, recv, d).start()

    def wait(ref, s):
        pltpu.make_async_copy(ref, ref, s).wait()

    h_dst = [dev(x, yh, z % 2, 2 * s + c, yl) for s in range(NK)]
    w_dst = [dev(2 * yh + z % 2, x // 2, x % 2, 2 * s + c, yl) for s in range(NK)]
    near = (0, 1, -1, 2, -2)
    c_dst = [(o, e, dev(2 * (x // 2) + e, yh, z % 2, (z + o + NZ) % NZ, c)) for o in near for e in range(2)]
    h_src = [dev(x, yh, c, 2 * k + yl, z % 2) for k in range(NK)]
    w_src = [dev(y, x // 2, c, 2 * k + x % 2, z % 2) for k in range(NK)]
    c_src = [(abs(o) % 2, dev(2 * (x // 2) + a, yh, b, (z + o + NZ) % NZ, c))
             for o in near for a in range(2) for b in range(2)]
    right, left = dev(x, yh, yl, (z + 1) % NZ, c), dev(x, yh, yl, (z + NZ - 1) % NZ, c)
    right2, left2 = dev(x, yh, yl, (z + 2) % NZ, c), dev(x, yh, yl, (z + NZ - 2) % NZ, c)
    sibling = dev(x, yh, yl, z, 1 - c)
    x_dst = [dev((x + o) % 4, yh, yl, z, c) for o in range(1, 4)]
    y_idx = [(y + o) % 4 for o in range(1, 4)]
    y_dst = [dev(x, v // 2, v % 2, z, c) for v in y_idx]

    loads = [pltpu.make_async_copy(a, b, sem_in.at[k])
             for k, (a, b) in enumerate([(gate_in, gate), (up_in, up), (cot_in, cot), (weight_in, weight)])]
    for load in loads:
        load.start()

    barrier = pltpu.get_barrier_semaphore()

    def greet(d):
        pl.semaphore_signal(barrier, inc=1, device_id=d, device_id_type=MESH)

    for d in h_src + w_src:
        @pl.when(jnp.logical_not(is_me(d)))
        def _():
            greet(d)
    for odd, d in c_src:
        @pl.when(jnp.logical_and(par == odd, jnp.logical_not(is_me(d))))
        def _():
            greet(d)
    for d in [right, left, right2, left2, sibling] + x_dst + y_dst:
        greet(d)

    loads[0].wait()
    loads[1].wait()
    for b in range(FD // 128):
        cols = slice(b * 128, (b + 1) * 128)
        g, u = gate[:, cols].astype(F32), up[:, cols].astype(F32)
        sig = jax.nn.sigmoid(g)
        act = g * sig
        hid_t[cols, :] = (act * u).T.astype(BF16)

    def others(dsts):
        n = jnp.int32(0)
        for d in dsts:
            n = n + jnp.where(is_me(d), 0, 1)
        return n

    loads[2].wait()
    loads[3].wait()
    n_h, n_w, n_c = others(h_dst), others(w_dst), others([d for _, _, d in c_dst])
    pl.semaphore_wait(barrier, n_h + n_w + n_c + 11)

    kz = z // 2

    def send_cot():
        for o, e, d in c_dst:
            send_any(cot.at[:, pl.ds(e * B, B)],
                     cot_b.at[c * 2 + x % 2, pl.ds((z // 2) * B, B), pl.ds(yl * B, B)],
                     sems["cot_send"], sem_near.at[o + 2], d)

    def send_weights(part):
        for s in part:
            send_any(weight.at[pl.ds(s * R, R)],
                     w_g.at[(kz % 2) * 2 + kz // 4, pl.ds(x * R, R), pl.ds(((kz // 2) % 2) * B, B)],
                     sems["w_send"], sem_w.at[kz], w_dst[s])

    send_cot()

    def send_hidden(part):
        for s in part:
            send_any(hid_t.at[pl.ds(s * R, R)],
                     h_g.at[kz // 2, pl.ds(x * R, R), pl.ds((kz % 2) * B, B)],
                     sems["h_send"], sem_h.at[kz], h_dst[s])

    for b in range(FD // 128):
        cols = slice(b * 128, (b + 1) * 128)
        g, u = gate[:, cols].astype(F32), up[:, cols].astype(F32)
        sig = jax.nn.sigmoid(g)
        f_up[:, cols] = g * sig
        f_gate[:, cols] = u * sig * (1.0 + g * (1.0 - sig))

    def panel(zt):
        return cot_b.at[pl.ds(2 * c, 2), pl.ds(((zt + 2 * NZ) % NZ) // 2 * B, B)]

    def forward(ref, d, send, recv):
        remote(ref, ref, send, recv, d).start()

    def piece(zt, q):
        return cot_b.at[pl.ds(2 * c, 2), pl.ds(((zt + 2 * NZ) % NZ) // 2 * B + q * PR, PR)]

    three = h_g.at[:, pl.ds(0, 3 * R)]

    def pass_weights():
        for q in range(NC):
            mine = w_g.at[q, pl.ds(y * R, R)]
            for a in range(2):
                wait(mine.at[:, pl.ds(a * B, B)], sem_w.at[(q % 2) * 4 + 2 * a + q // 2])
            for d in y_dst:
                forward(mine, d, sems["wg_send"], sems["wg_recv"])

    def pass_hidden():
        for q in range(NC):
            mine = h_g.at[q, pl.ds(x * R, R)]
            for a in range(2):
                wait(mine.at[:, pl.ds(a * B, B)], sem_h.at[2 * q + a])
            for d in x_dst:
                forward(mine, d, sems["hg_send"], sems["hg_recv"])

    def to_sibling(zt):
        forward(panel(zt), sibling, sems["sib_send"], sems["sib_recv"])

    def act(point):
        for what in PLAN[point]:
            if what == "pass_w":
                pass_weights()
            elif what == "pass_h":
                pass_hidden()
            else:
                (send_weights if what[0] == "w" else send_hidden)(what[1])

    act(0)

    def hand_on(zt, d, q, one, two, send, recv):
        forward(piece(zt, q), two, send, recv.at[(d + 2) * NP + q]) if two is not None else None
        forward(piece(zt, q), one, send, recv.at[(d + 1) * NP + q])

    for t in range(4):
        @pl.when(par == 0)
        def _():
            d = 2 * t + 2
            if t == 0:
                wait(panel(z - 2), sem_near.at[4])
                wait(panel(z + 2), sem_near.at[0])
            for q in range(NP):
                if t > 0:
                    wait(piece(z - d, q), sem_ring_r.at[d * NP + q])
                if t < 3:
                    hand_on(z - d, d, q, right, right2, sems["ring_send_r"], sem_ring_r)
                    if t > 0:
                        wait(piece(z + d, q), sem_ring_l.at[d * NP + q])
                    hand_on(z + d, d, q, left, left2 if t < 2 else None, sems["ring_send_l"], sem_ring_l)
            to_sibling(z - d)
            if t < 3:
                to_sibling(z + d)
            if t == 0:
                wait(panel(z), sem_near.at[2])
                to_sibling(z)

        @pl.when(par == 1)
        def _():
            d = 2 * t + 1
            if t == 0:
                wait(panel(z - 1), sem_near.at[3])
                wait(panel(z + 1), sem_near.at[1])
            else:
                for q in range(NP):
                    wait(piece(z - d, q), sem_ring_r.at[d * NP + q])
                    wait(piece(z + d, q), sem_ring_l.at[d * NP + q])
            to_sibling(z - d)
            to_sibling(z + d)

        act(t + 1)

    wait(cot_b.at[pl.ds(2 * (1 - c), 2)], sems["sib_recv"])
    wait(three, sems["wg_recv"])

    def multiply_dhid(n):
        total = jnp.zeros((RS, CH), F32)
        for q in range(NC):
            total += lax.dot_general(w_g[q], cot_b[q, n * CH:(n + 1) * CH, :], (((1,), (1,)), ((), ())),
                                     preferred_element_type=F32)
        d_f[n] = total
        for v in range(NX):
            d_p[v, n] = total[v * R:(v + 1) * R].astype(GRAD_SUM)
        for o in range(1, 4):
            remote(d_p.at[(x + o) % 4, n], d_r.at[o - 1, n], sems["ds_send"], sem_d.at[n], x_dst[o - 1]).start()

    def multiply_down(n):
        total = jnp.zeros((RS, CH), F32)
        for q in range(NC):
            total += jnp.dot(h_g[q], cot_b[n, q * CH:(q + 1) * CH, :], preferred_element_type=F32)
        g_f[n] = total
        for v in range(NX):
            g_p[v, n] = total[v * R:(v + 1) * R].astype(DOWN_SUM)
        for o in range(1, 4):
            remote(g_p.at[y_idx[o - 1], n], g_r.at[o - 1, n], sems["gs_send"], sem_g.at[n], y_dst[o - 1]).start()

    back = pl.ds(pl.multiple_of((z // 2) * R, R), R)

    def reduce_dhid(n):
        wait(d_r.at[:, n], sem_d.at[n])
        total = d_f[n, pl.ds(pl.multiple_of(x * R, R), R), :]
        for o in range(3):
            total += d_r[o, n].astype(F32)
        for a in range(2):
            k = 2 * n + a
            d_s[k] = total[:, a * B:(a + 1) * B].astype(GRAD_BACK)
            send_any(d_s.at[k], d_own.at[back], sems["db_send"], sems["db_recv"], h_src[k])

    def reduce_down(n):
        wait(g_r.at[:, n], sem_g.at[n])
        total = g_f[n, pl.ds(pl.multiple_of(y * R, R), R), :]
        for o in range(3):
            total += g_r[o, n].astype(F32)
        for a in range(2):
            k = 4 * (n % 2) + 2 * a + n // 2
            g_s[k] = total[:, a * B:(a + 1) * B].astype(DOWN_BACK)
            send_any(g_s.at[k], g_own.at[back], sems["gb_send"], sems["gb_recv"], w_src[k])

    wait(three, sems["hg_recv"])
    for n in range(NC + AHEAD):
        if n < NC:
            multiply_dhid(n)
            multiply_down(n)
        if n >= AHEAD:
            reduce_dhid(n - AHEAD)
            reduce_down(n - AHEAD)

    wait(d_own, sems["db_recv"])
    for b in range(FD // 128):
        cols = slice(b * 128, (b + 1) * 128)
        dhid = d_own[cols, :].astype(F32).T
        o_up[:, cols] = (dhid * f_up[:, cols]).astype(BF16)
        o_gate[:, cols] = (dhid * f_gate[:, cols]).astype(BF16)
    wait(g_own, sems["gb_recv"])
    scale = 1.0 / 64.0
    o_down[...] = g_own[...].astype(F32) * scale

    def wait_all(ref, s, count, most):
        for k in (most - 1, most):
            @pl.when(count == k)
            def _():
                wait(ref.at[pl.ds(0, k)], s)

    def wait_rows(ref, s, count):
        for k in (NK - 1, NK):
            @pl.when(count == k)
            def _():
                wait(ref.at[pl.ds(0, k * R)], s)

    for k in (0, 1):
        @pl.when(n_c == len(c_dst) - k)
        def _():
            wait(cot_b.at[0, pl.ds(0, (len(c_dst) - k) // 2 * B)], sems["cot_send"])
            if k:
                wait(cot.at[:, pl.ds(0, B)], sems["cot_send"])
    wait_rows(weight, sems["w_send"], n_w)
    wait_rows(hid_t, sems["h_send"], n_h)

    @pl.when(par == 0)
    def _():
        wait(cot_b.at[pl.ds(0, 2), pl.ds(0, 6 * B)], sems["ring_send_r"])
        wait(cot_b.at[pl.ds(0, 2), pl.ds(0, 5 * B)], sems["ring_send_l"])

    wait(cot_b.at[pl.ds(0, 2)], sems["sib_send"])
    wait(three, sems["wg_send"])
    wait(three, sems["hg_send"])
    wait(d_r, sems["ds_send"])
    wait(g_r, sems["gs_send"])
    wait_all(d_s, sems["db_send"], n_h, NK)
    wait_all(g_s, sems["gb_send"], n_w, NK)


def shards(cotangent, gate_pre, up_pre, down_weight):
    vmem = pl.BlockSpec(memory_space=pltpu.VMEM)
    dma = pltpu.SemaphoreType.DMA
    return pl.pallas_call(
        kernel,
        name="swiglu_down_backward",
        out_shape=(
            jax.ShapeDtypeStruct((B, FD), BF16),
            jax.ShapeDtypeStruct((B, FD), BF16),
            jax.ShapeDtypeStruct((FD, B), F32),
        ),
        in_specs=[pl.BlockSpec(memory_space=pltpu.HBM)] * 4,
        out_specs=(vmem,) * 3,
        scratch_shapes=[
            pltpu.VMEM((B, 2 * B), BF16),
            pltpu.VMEM((B, FD), BF16),
            pltpu.VMEM((B, FD), BF16),
            pltpu.VMEM((FD, B), BF16),
            pltpu.VMEM((FD, B), BF16),
            pltpu.VMEM((B, FD), F32),
            pltpu.VMEM((B, FD), F32),
            pltpu.VMEM((NC, NK * B, CH), BF16),
            pltpu.VMEM((NC, RS, CH), BF16),
            pltpu.VMEM((NC, RS, CH), BF16),
            pltpu.VMEM((NC, RS, CH), F32),
            pltpu.VMEM((NX, NC, R, CH), GRAD_SUM),
            pltpu.VMEM((3, NC, R, CH), GRAD_SUM),
            pltpu.VMEM((NK, R, B), GRAD_BACK),
            pltpu.VMEM((FD, B), GRAD_BACK),
            pltpu.VMEM((NC, RS, CH), F32),
            pltpu.VMEM((NX, NC, R, CH), DOWN_SUM),
            pltpu.VMEM((3, NC, R, CH), DOWN_SUM),
            pltpu.VMEM((NK, R, B), DOWN_BACK),
            pltpu.VMEM((FD, B), DOWN_BACK),
            dma((5,)), dma((9 * NP,)), dma((8 * NP,)), dma((NK,)), dma((NK,)), dma((NC,)), dma((NC,)), dma((4,)), dma((17,)),
        ],
        compiler_params=pltpu.CompilerParams(
            collective_id=0, has_side_effects=True, vmem_limit_bytes=60 * 2**20),
        cost_estimate=pl.CostEstimate(flops=4 * RS * 1024 * 1024, bytes_accessed=2 * 2**20, transcendentals=B * FD),
    )(cotangent, gate_pre, up_pre, down_weight)


def solution(mesh):
    in_specs = (P("dp", "tensor"), P("dp", "tensor"), P("dp", "tensor"), P("tensor", "dp"))
    out_specs = (P("dp", "tensor"), P("dp", "tensor"), P("tensor", "dp"))
    return jax.shard_map(shards, mesh=mesh, in_specs=in_specs, out_specs=out_specs, check_vma=False)
```
